768 devices in a mesh: outer: 8 (over y_lo, core), inner: 96 (over z, x, y_hi).
Axes of the slice: x: 4, y: 8 (y_hi: 2, y_lo: 4; y = y_hi * 4 + y_lo), z: 12, core: 2. Of those that a mesh axis runs over, the one named last changes fastest.
Arguments:
- image_emb: bfloat16 [196608, 1152], P(('outer', 'inner')), may hold values from -0.3 to 0.3
- text_emb: bfloat16 [196608, 1152], P(('outer', 'inner')), may hold values from -0.3 to 0.3
- positive: int32 [196608], P(('outer', 'inner')), may hold values from 0 to 196607, as said below
- log_scale: float32 [1], replicated, may hold values from 1.8 to 2.5
- logit_bias: float32 [1], replicated, may hold values from -3 to -1
Outputs:
- image_grad: float32 [196608, 1152], P(('outer', 'inner'))
- text_grad: float32 [196608, 1152], P(('outer', 'inner'))
- loss: float32 [1], replicated
- head_grad: float32 [2], replicated
The draws below stay inside these ranges and needn't reach their ends.
Inputs may be any that keep to these rules, and one draw needn't show every extreme that they name: `positive`: each image's matching text lies in one of the text blocks that the image is scored against.
All inputs are finite; a program needn't handle non-finite values.
Results may differ from the reference program's by a relative error of at most 0.00047.
Values may be sent and summed in bfloat16 or wider, within the bound.
No kernel may reach another device: no remote copies, remote signals or barrier semaphores. Data moves between devices by JAX's collectives and lax.ppermute only.
A program may use at most 32 MiB of HBM per device.

```python
import jax
import jax.numpy as jnp
from jax import lax

D = 1152
ROWS = 256
IN_SPAN = 3
BATCH = 196608
N_OUTER = 8
N_INNER = 96


def shared_line(key):
    line = jax.random.normal(jax.random.fold_in(key, 97), (D,), dtype=jnp.float32)
    return jnp.clip(line, -3.0, 3.0)


def block_amplitude(key, top):
    block_count = N_OUTER * N_INNER
    blocks = jnp.arange(block_count, dtype=jnp.int32).astype(jnp.float32)
    rising = 0.25 + 0.75 * blocks / jnp.float32(block_count - 1)
    factor = jax.random.uniform(key, (block_count,), jnp.float32, 0.2, 1.0)
    return jnp.repeat(top * rising * factor, ROWS)


def embed_rows(key, line, top):
    row_total = ROWS * N_OUTER * N_INNER
    key_noise = jax.random.fold_in(key, 0)
    key_amp = jax.random.fold_in(key, 2)
    noise = jnp.clip(0.03 * jax.random.normal(key_noise, (row_total, D), dtype=jnp.float32), -0.2, 0.2)
    amplitude = block_amplitude(key_amp, top)
    values = noise + 0.03 * amplitude[:, None] * line[None, :]
    return values


def draw_image_emb(key, part):
    line = shared_line(key)
    key = jax.random.fold_in(key, 21)
    values = embed_rows(key, line, 0.8)
    return values.astype(jnp.bfloat16)


def draw_text_emb(key, part):
    line = shared_line(key)
    key = jax.random.fold_in(key, 33)
    values = embed_rows(key, line, 0.8)
    return values.astype(jnp.bfloat16)


def draw_positive(key, part):
    key = jax.random.fold_in(key, 11)
    key_outer, key_inner, key_row = jax.random.split(key, 3)
    row_total = ROWS * N_OUTER * N_INNER
    row_ids = jnp.arange(row_total, dtype=jnp.int32)
    device_id = row_ids // ROWS
    outer_pos = device_id // N_INNER
    inner_pos = device_id % N_INNER
    outer_off = jax.random.randint(key_outer, (row_total,), 0, 2, dtype=jnp.int32)
    inner_off = jax.random.randint(key_inner, (row_total,), 0, IN_SPAN, dtype=jnp.int32)
    row_pick = jax.random.randint(key_row, (row_total,), 0, ROWS, dtype=jnp.int32)
    owner_id = (outer_pos - outer_off) % N_OUTER * N_INNER + (inner_pos - inner_off) % N_INNER
    return (owner_id * ROWS + row_pick).astype(jnp.int32)


def setup_inputs(seed: int = 0) -> dict:
    key_list = jax.random.split(jax.random.key(seed), 6)
    image_emb = draw_image_emb(jax.random.fold_in(key_list[5], 71), 0)
    text_emb = draw_text_emb(jax.random.fold_in(key_list[5], 71), 0)
    positive = draw_positive(jax.random.fold_in(key_list[5], 71), 0)
    log_scale = jnp.clip(jax.random.uniform(key_list[3], (1,), jnp.float32, 1.8, 2.5), 1.8, 2.5)
    logit_bias = jnp.clip(jax.random.uniform(key_list[4], (1,), jnp.float32, -3.0, -1.0), -3.0, -1.0)
    return dict(image_emb=image_emb, text_emb=text_emb, positive=positive, log_scale=log_scale, logit_bias=logit_bias)


NORM_EPS = 1e-06

def normalize(values):
    values32 = values.astype(jnp.float32)
    inv_norm = lax.rsqrt(lax.optimization_barrier(jnp.sum(values32 * values32, axis=-1, keepdims=True)) + NORM_EPS)
    return (values32 * inv_norm, inv_norm)

def unnormalize(unit32, inv_norm, grad_unit):
    return inv_norm * (grad_unit - unit32 * lax.optimization_barrier(jnp.sum(unit32 * grad_unit, axis=-1, keepdims=True)))

def score_tile(img_unit, txt_unit, matches, text_start, temp_scale, bias_value):
    cosine = jnp.dot(img_unit, txt_unit.T, preferred_element_type=jnp.float32)
    logit = temp_scale * cosine + bias_value
    text_ids = text_start + jnp.arange(txt_unit.shape[0], dtype=jnp.int32)
    labels = jnp.where(matches[:, None] == text_ids[None, :], 1.0, -1.0).astype(jnp.float32)
    margin = labels * logit
    tile_loss = jnp.sum(jax.nn.softplus(-margin))
    slope = -labels * jax.nn.sigmoid(-margin)
    weights = slope.astype(jnp.bfloat16)
    img_part = jnp.dot(weights, txt_unit, preferred_element_type=jnp.float32)
    txt_part = jnp.dot(weights.T, img_unit, preferred_element_type=jnp.float32)
    return (tile_loss, jnp.sum(slope * cosine), jnp.sum(slope), img_part, txt_part)

def take_block(values, device_id):
    return lax.dynamic_slice_in_dim(values, (device_id * ROWS).astype(jnp.int32), ROWS, 0)

def reference(image_emb, text_emb, positive, log_scale, logit_bias):
    temp_scale = jnp.exp(log_scale[0])
    bias_value = logit_bias[0]
    img_unit32, img_inv = normalize(image_emb)
    txt_unit32, txt_inv = normalize(text_emb)
    img_unit = img_unit32.astype(jnp.bfloat16)
    txt_unit = txt_unit32.astype(jnp.bfloat16)
    offsets = [(outer_off, inner_off) for outer_off in range(2) for inner_off in range(IN_SPAN)]

    def image_side(device_id):
        outer_pos = device_id // N_INNER
        inner_pos = device_id % N_INNER
        img_total = jnp.zeros((ROWS, D), jnp.float32)
        tile_stats = jnp.zeros((3,), jnp.float32)
        for outer_off, inner_off in offsets:
            owner_id = (outer_pos - outer_off) % N_OUTER * N_INNER + (inner_pos - inner_off) % N_INNER
            tile_loss, slope_cos, slope_sum, img_part, txt_part = score_tile(take_block(img_unit, device_id), take_block(txt_unit, owner_id), take_block(positive, device_id), (owner_id * ROWS).astype(jnp.int32), temp_scale, bias_value)
            img_total = img_total + img_part
            tile_stats = tile_stats + jnp.stack([tile_loss, slope_cos, slope_sum])
        return (img_total, tile_stats)

    def text_side(device_id):
        outer_pos = device_id // N_INNER
        inner_pos = device_id % N_INNER
        txt_total = jnp.zeros((ROWS, D), jnp.float32)
        for outer_off, inner_off in offsets:
            source_id = (outer_pos + outer_off) % N_OUTER * N_INNER + (inner_pos + inner_off) % N_INNER
            tile_loss, slope_cos, slope_sum, img_part, txt_part = score_tile(take_block(img_unit, source_id), take_block(txt_unit, device_id), take_block(positive, source_id), (device_id * ROWS).astype(jnp.int32), temp_scale, bias_value)
            txt_total = txt_total + txt_part
        return txt_total
    device_ids = jnp.arange(N_OUTER * N_INNER, dtype=jnp.int32)
    img_blocks, tile_stats = lax.map(image_side, device_ids)
    txt_blocks = lax.map(text_side, device_ids)
    img_dz = temp_scale * img_blocks.reshape(BATCH, D)
    txt_dz = temp_scale * txt_blocks.reshape(BATCH, D)
    image_grad = unnormalize(img_unit32, img_inv, img_dz)
    text_grad = unnormalize(txt_unit32, txt_inv, txt_dz)
    totals = lax.optimization_barrier(jnp.sum(tile_stats, axis=0))
    pair_count = jnp.float32(BATCH * 2 * IN_SPAN * ROWS)
    loss = (totals[0] / pair_count).reshape(1)
    head_grad = jnp.stack([temp_scale * totals[1], totals[2]]) / pair_count
    return (image_grad, text_grad, loss, head_grad)
```

```python
import functools

import jax
import jax.numpy as jnp
from jax import lax
from jax.experimental import pallas as pl
from jax.experimental.pallas import tpu as pltpu
from jax.sharding import PartitionSpec as P

IN_SPAN = 3
NORM_EPS = 1e-06
AXES = ("outer", "inner")
SEND_SCALE = 64.0
VMEM_LIMIT = 48 * 1024 * 1024


def moved(block, outer_step, inner_step):
    n_outer, n_inner = lax.axis_size("outer"), lax.axis_size("inner")
    route = [
        (o * n_inner + p, (o + outer_step) % n_outer * n_inner + (p + inner_step) % n_inner)
        for o in range(n_outer)
        for p in range(n_inner)
    ]
    return lax.ppermute(block, AXES, route)


def unit_of(ref):
    values = ref[...].astype(jnp.float32)
    inv = lax.rsqrt(jnp.sum(values * values, axis=-1, keepdims=True) + NORM_EPS)
    return (values * inv).astype(jnp.bfloat16)


def score(img, txt, pos, text_start, head, stats):
    cosine = lax.dot_general(
        img, txt, (((1,), (1,)), ((), ())), preferred_element_type=jnp.float32
    )
    logit = head[0] * cosine + head[1]
    ids = text_start + lax.broadcasted_iota(jnp.int32, cosine.shape, 1)
    hit = pos == ids
    z = jnp.where(hit, -logit, logit)
    tail = jnp.exp(-jnp.abs(z))
    loss = jnp.maximum(z, 0.0) + jnp.log1p(tail)
    sig = jnp.where(z >= 0.0, 1.0, tail) / (1.0 + tail)
    slope = jnp.where(hit, -sig, sig)
    for row, term in enumerate((loss, slope * cosine, slope)):
        col = jnp.sum(term, axis=0, keepdims=True)
        width = stats.shape[1]
        part = col[:, :width]
        for at in range(width, col.shape[1], width):
            part = part + col[:, at : at + width]
        stats[row : row + 1, :] += part
    return slope.astype(jnp.bfloat16)


def times(a, b):
    return jnp.dot(a, b, preferred_element_type=jnp.float32)


def times_t(a, b):
    return lax.dot_general(a, b, (((0,), (0,)), ((), ())), preferred_element_type=jnp.float32)


def first_kernel(head, start, img_raw, txt_raw, pos, img_u, txt_u, img_acc, txt_acc, stats):
    stats[...] = jnp.zeros_like(stats)
    img_u[...] = unit_of(img_raw)
    txt_u[...] = unit_of(txt_raw)
    s = score(img_u[...], txt_u[...], pos[...], start[0], head, stats)
    img_acc[...] = times(s, txt_u[...])
    txt_acc[...] = times_t(s, img_u[...])


def second_kernel(
    head, start, img_u, txt_u, far_raw, img2_raw, pos, pos2, img_in, txt_in, stats_in,
    img2_u, img_acc, img2_acc, txt_acc, far_acc, stats,
):
    stats[...] = stats_in[...]
    img2_u[...] = unit_of(img2_raw)
    far = unit_of(far_raw)
    s = score(img_u[...], far, pos[...], start[2], head, stats)
    s2 = score(img2_u[...], far, pos2[...], start[2], head, stats)
    s0 = score(img2_u[...], txt_u[...], pos2[...], start[0], head, stats)
    far_acc[...] = times_t(s, img_u[...]) + times_t(s2, img2_u[...])
    img_acc[...] = img_in[...] + times(s, far)
    img2_acc[...] = times(s2, far) + times(s0, txt_u[...])
    txt_acc[...] = txt_in[...] + times_t(s0, img2_u[...])


def third_kernel(
    head, start, img_u, img2_u, mid_raw, pos, pos2, img_in, img2_in, stats_in,
    img_acc, img2_acc, mid_acc, stats,
):
    stats[...] = stats_in[...]
    mid = unit_of(mid_raw)
    s = score(img_u[...], mid, pos[...], start[1], head, stats)
    s2 = score(img2_u[...], mid, pos2[...], start[1], head, stats)
    mid_acc[...] = SEND_SCALE * (times_t(s, img_u[...]) + times_t(s2, img2_u[...]))
    img_acc[...] = img_in[...] + times(s, mid)
    img2_acc[...] = SEND_SCALE * (img2_in[...] + times(s2, mid))


def finish(raw, total, temp):
    values = raw[...].astype(jnp.float32)
    inv = lax.rsqrt(jnp.sum(values * values, axis=-1, keepdims=True) + NORM_EPS)
    unit = values * inv
    grad = temp * total
    return inv * (grad - unit * jnp.sum(unit * grad, axis=-1, keepdims=True))


def call(kernel, ins, outs):
    scalars = [pl.BlockSpec(memory_space=pltpu.SMEM)] * 2
    arrays = [pl.BlockSpec(memory_space=pltpu.VMEM)] * (len(ins) - 2)
    return pl.pallas_call(
        kernel,
        in_specs=scalars + arrays,
        out_specs=[pl.BlockSpec(memory_space=pltpu.VMEM)] * len(outs),
        out_shape=outs,
        compiler_params=pltpu.CompilerParams(vmem_limit_bytes=VMEM_LIMIT),
    )(*ins)


def total_over_devices(s):
    n_outer, n_inner = lax.axis_size("outer"), lax.axis_size("inner")
    step = n_outer // 2
    while step:
        s = s + moved(s, step, 0)
        step //= 2
    third = n_inner // 3
    group = lax.axis_index("inner") // third
    parts = [s, moved(s, 0, third), moved(s, 0, 2 * third)]
    ordered = [
        jnp.where(group == g, parts[0], jnp.where((group - 1) % 3 == g, parts[1], parts[2]))
        for g in range(3)
    ]
    s = ordered[0] + ordered[1] + ordered[2]
    step = third // 2
    while step:
        s = s + moved(s, 0, step)
        step //= 2
    return s


def shards(image_emb, text_emb, positive, log_scale, logit_bias):
    rows, width = image_emb.shape
    n_outer, n_inner = lax.axis_size("outer"), lax.axis_size("inner")
    f32, bf16 = jnp.float32, jnp.bfloat16
    temp_scale = jnp.exp(log_scale[0])
    head = jnp.stack([temp_scale, logit_bias[0]])
    outer_pos, inner_pos = lax.axis_index("outer"), lax.axis_index("inner")
    start = jnp.stack(
        [(outer_pos * n_inner + (inner_pos - b) % n_inner) * rows for b in range(IN_SPAN)]
    ).astype(jnp.int32)
    pos = positive.reshape(rows, 1)

    mid_raw = moved(text_emb, 0, 1)
    img2_raw = moved(image_emb, -1, 0)
    far_raw = moved(text_emb, 0, 2)
    pos2 = moved(positive, -1, 0).reshape(rows, 1)

    wide = jax.ShapeDtypeStruct((rows, width), f32)
    unit = jax.ShapeDtypeStruct((rows, width), bf16)
    sums = jax.ShapeDtypeStruct((8, 128), f32)
    img_u, txt_u, img_acc, txt_acc, stats = call(
        first_kernel, (head, start, image_emb, text_emb, pos), [unit, unit, wide, wide, sums]
    )
    img2_u, img_acc, img2_acc, txt_acc, far_acc, stats = call(
        second_kernel,
        (head, start, img_u, txt_u, far_raw, img2_raw, pos, pos2, img_acc, txt_acc, stats),
        [unit, wide, wide, wide, wide, sums],
    )
    far_back = moved(far_acc, 0, -2)
    img_acc, img2_acc, mid_acc, stats = call(
        third_kernel,
        (head, start, img_u, img2_u, mid_raw, pos, pos2, img_acc, img2_acc, stats),
        [wide, wide, wide, sums],
    )
    mid_back = moved(mid_acc.astype(jnp.float16), 0, -1)
    img_back = moved(img2_acc.astype(jnp.float16), 1, 0)
    totals = jnp.sum(total_over_devices(stats), axis=1)

    img_total = img_acc + img_back.astype(f32) * (1.0 / SEND_SCALE)
    txt_total = txt_acc + far_back + mid_back.astype(f32) * (1.0 / SEND_SCALE)
    image_grad = finish(image_emb, img_total, temp_scale)
    text_grad = finish(text_emb, txt_total, temp_scale)
    pair_count = f32(rows * n_outer * n_inner * 2 * IN_SPAN * rows)
    loss = (totals[0] / pair_count).reshape(1)
    head_grad = jnp.stack([temp_scale * totals[1], totals[2]]) / pair_count
    return (image_grad, text_grad, loss, head_grad)


def solution(mesh):
    return jax.shard_map(
        shards,
        mesh=mesh,
        in_specs=(P(AXES, None), P(AXES, None), P(AXES), P(), P()),
        out_specs=(P(AXES, None), P(AXES, None), P(), P()),
        check_vma=False,
    )
```

```python
import jax
import jax.numpy as jnp
from jax import lax
from jax.experimental import pallas as pl
from jax.experimental.pallas import tpu as pltpu
from jax.sharding import Mesh
from jax.sharding import PartitionSpec as P

IN_SPAN = 3
NORM_EPS = 1e-06
AXES = ("y_lo", "core", "z", "x", "y_hi")
SIZES = (4, 2, 12, 4, 2)
N_OUTER, N_INNER = 8, 96
SEND_SCALE = 64.0
VMEM_LIMIT = 24 * 1024 * 1024


def moved(block, outer_step, inner_step):
    route = [
        (o * N_INNER + p, (o + outer_step) % N_OUTER * N_INNER + (p + inner_step) % N_INNER)
        for o in range(N_OUTER)
        for p in range(N_INNER)
    ]
    return lax.ppermute(block, AXES, route)


def unit_of(ref):
    values = ref[...].astype(jnp.float32)
    inv = lax.rsqrt(jnp.sum(values * values, axis=-1, keepdims=True) + NORM_EPS)
    return (values * inv).astype(jnp.bfloat16)


def score(img, txt, pos, text_start, head, stats):
    cosine = lax.dot_general(
        img, txt, (((1,), (1,)), ((), ())), preferred_element_type=jnp.float32
    )
    logit = head[0] * cosine + head[1]
    ids = text_start + lax.broadcasted_iota(jnp.int32, cosine.shape, 1)
    hit = pos == ids
    z = jnp.where(hit, -logit, logit)
    tail = jnp.exp(-jnp.abs(z))
    loss = jnp.maximum(z, 0.0) + jnp.log1p(tail)
    sig = jnp.where(z >= 0.0, 1.0, tail) / (1.0 + tail)
    slope = jnp.where(hit, -sig, sig)
    for row, term in enumerate((loss, slope * cosine, slope)):
        col = jnp.sum(term, axis=0, keepdims=True)
        width = stats.shape[1]
        part = col[:, :width]
        for at in range(width, col.shape[1], width):
            part = part + col[:, at : at + width]
        stats[row : row + 1, :] += part
    return slope.astype(jnp.bfloat16)


def times(a, b):
    return jnp.dot(a, b, preferred_element_type=jnp.float32)


def times_t(a, b):
    return lax.dot_general(a, b, (((0,), (0,)), ((), ())), preferred_element_type=jnp.float32)


def unit_kernel(head, start, img_raw, txt_raw, img_u, txt_u):
    img_u[...] = unit_of(img_raw)
    txt_u[...] = unit_of(txt_raw)


def first_kernel(head, start, img_u, txt_u, pos, img_acc, txt_acc, stats):
    stats[...] = jnp.zeros_like(stats)
    s = score(img_u[...], txt_u[...], pos[...], start[0], head, stats)
    img_acc[...] = times(s, txt_u[...])
    txt_acc[...] = times_t(s, img_u[...])


def second_kernel(
    head, start, img_u, txt_u, far_u, img2_u, pos, pos2, img_in, txt_in, stats_in,
    img_acc, img2_acc, txt_acc, far_acc, stats,
):
    stats[...] = stats_in[...]
    s = score(img_u[...], far_u[...], pos[...], start[2], head, stats)
    s2 = score(img2_u[...], far_u[...], pos2[...], start[2], head, stats)
    s0 = score(img2_u[...], txt_u[...], pos2[...], start[0], head, stats)
    far_acc[...] = times_t(s, img_u[...]) + times_t(s2, img2_u[...])
    img_acc[...] = img_in[...] + times(s, far_u[...])
    img2_acc[...] = times(s2, far_u[...]) + times(s0, txt_u[...])
    txt_acc[...] = txt_in[...] + times_t(s0, img2_u[...])


def third_kernel(head, start, img_u, img2_u, mid_raw, pos, pos2, stats_in, mid_u, slope, slope2, mid_acc, stats):
    stats[...] = stats_in[...]
    mid = unit_of(mid_raw)
    mid_u[...] = mid
    s = score(img_u[...], mid, pos[...], start[1], head, stats)
    s2 = score(img2_u[...], mid, pos2[...], start[1], head, stats)
    slope[...] = s
    slope2[...] = s2
    total = times_t(s, img_u[...]) + times_t(s2, img2_u[...])
    mid_acc[...] = SEND_SCALE * total


def fourth_kernel(head, start, mid_u, slope, slope2, img_in, img2_in, img_acc, img2_acc):
    img_acc[...] = img_in[...] + times(slope[...], mid_u[...])
    total = img2_in[...] + times(slope2[...], mid_u[...])
    img2_acc[...] = SEND_SCALE * total


def finish_kernel(head, start, img_raw, txt_raw, img_total, txt_total, img_grad, txt_grad):
    for raw, total, out in ((img_raw, img_total, img_grad), (txt_raw, txt_total, txt_grad)):
        values = raw[...].astype(jnp.float32)
        inv = lax.rsqrt(jnp.sum(values * values, axis=-1, keepdims=True) + NORM_EPS)
        unit = values * inv
        grad = head[0] * total[...]
        out[...] = inv * (grad - unit * jnp.sum(unit * grad, axis=-1, keepdims=True))


def call(kernel, ins, outs):
    scalars = [pl.BlockSpec(memory_space=pltpu.SMEM)] * 2
    arrays = [pl.BlockSpec(memory_space=pltpu.VMEM)] * (len(ins) - 2)
    return pl.pallas_call(
        kernel,
        in_specs=scalars + arrays,
        out_specs=[pl.BlockSpec(memory_space=pltpu.VMEM)] * len(outs),
        out_shape=outs,
        compiler_params=pltpu.CompilerParams(vmem_limit_bytes=VMEM_LIMIT),
    )(*ins)


def sum_first(s):
    s = lax.psum(lax.psum(s, ("y_lo", "core")), "y_hi")
    return jnp.sum(lax.all_gather(s, "z"), axis=0)


def sum_last(s):
    s = s + moved(s, 0, 4)
    return s + moved(s, 0, 2)


def shards(image_emb, text_emb, positive, log_scale, logit_bias):
    rows, width = image_emb.shape
    f32, bf16 = jnp.float32, jnp.bfloat16
    temp_scale = jnp.exp(log_scale[0])
    head = jnp.stack([temp_scale, logit_bias[0]])
    device = lax.axis_index(AXES)
    outer_pos, inner_pos = device // N_INNER, device % N_INNER
    start = jnp.stack(
        [(outer_pos * N_INNER + (inner_pos - b) % N_INNER) * rows for b in range(IN_SPAN)]
    ).astype(jnp.int32)
    pos = positive.reshape(rows, 1)
    wide = jax.ShapeDtypeStruct((rows, width), f32)
    unit = jax.ShapeDtypeStruct((rows, width), bf16)
    pair = jax.ShapeDtypeStruct((rows, rows), bf16)
    sums = jax.ShapeDtypeStruct((8, 128), f32)

    mid_raw = moved(text_emb, 0, 1)
    pos2 = moved(positive, -1, 0).reshape(rows, 1)
    img_u, txt_u = call(unit_kernel, (head, start, image_emb, text_emb), [unit, unit])
    img2_u = moved(img_u, -1, 0)
    far_u = moved(txt_u, 0, 2)
    img_acc, txt_acc, stats = call(
        first_kernel, (head, start, img_u, txt_u, pos), [wide, wide, sums]
    )
    img_acc, img2_acc, txt_acc, far_acc, stats = call(
        second_kernel,
        (head, start, img_u, txt_u, far_u, img2_u, pos, pos2, img_acc, txt_acc, stats),
        [wide, wide, wide, wide, sums],
    )
    far_back = moved(far_acc, 0, -2)
    mid_u, slope, slope2, mid_acc, stats = call(
        third_kernel,
        (head, start, img_u, img2_u, mid_raw, pos, pos2, stats),
        [unit, pair, pair, wide, sums],
    )
    mid_back = moved(mid_acc.astype(jnp.float16), 0, -1)
    img_acc, img2_acc = call(
        fourth_kernel,
        (head, start, mid_u, slope, slope2, img_acc, img2_acc),
        [wide, wide],
    )
    img_back = moved(img2_acc.astype(jnp.float16), 1, 0)
    always = lax.optimization_barrier(jnp.bool_(True))
    stats = lax.cond(always, sum_first, jnp.zeros_like, stats)
    stats, far_back, mid_back, img_back = lax.optimization_barrier(
        (stats, far_back, mid_back, img_back)
    )
    totals = jnp.sum(sum_last(stats), axis=1)

    img_total = img_acc + img_back.astype(f32) * (1.0 / SEND_SCALE)
    txt_total = txt_acc + far_back + mid_back.astype(f32) * (1.0 / SEND_SCALE)
    image_grad, text_grad = call(
        finish_kernel,
        (head, start, image_emb, text_emb, img_total, txt_total),
        [wide, wide],
    )
    pair_count = f32(rows * N_OUTER * N_INNER * 2 * IN_SPAN * rows)
    loss = (totals[0] / pair_count).reshape(1)
    head_grad = jnp.stack([temp_scale * totals[1], totals[2]]) / pair_count
    return (image_grad, text_grad, loss, head_grad)


def solution(mesh):
    fine = Mesh(mesh.devices.reshape(SIZES), AXES)
    return jax.shard_map(
        shards,
        mesh=fine,
        in_specs=(P(AXES, None), P(AXES, None), P(AXES), P(), P()),
        out_specs=(P(AXES, None), P(AXES, None), P(), P()),
        check_vma=False,
    )
```

```python
import jax
import jax.numpy as jnp
from jax import lax
from jax.experimental import pallas as pl
from jax.experimental.pallas import tpu as pltpu
from jax.sharding import Mesh
from jax.sharding import PartitionSpec as P

IN_SPAN = 3
NORM_EPS = 1e-06
AXES = ("y_lo", "core", "z", "x", "y_hi")
SIZES = (4, 2, 12, 4, 2)
N_OUTER, N_INNER = 8, 96
SEND_SCALE = 64.0
VMEM_LIMIT = 24 * 1024 * 1024


def moved(block, outer_step, inner_step):
    route = [
        (o * N_INNER + p, (o + outer_step) % N_OUTER * N_INNER + (p + inner_step) % N_INNER)
        for o in range(N_OUTER)
        for p in range(N_INNER)
    ]
    return lax.ppermute(block, AXES, route)


def half_way():
    route = []
    for device in range(N_OUTER * N_INNER):
        o, p = divmod(device, N_INNER)
        y = p % 2 * 4 + o // 2
        y = (y + (2 if o % 2 == 0 else 6)) % 8
        route.append((device, (y % 4 * 2 + o % 2) * N_INNER + p // 2 * 2 + y // 4))
    return route


def one_step_in_two(block, sign):
    first = half_way()
    ends = [
        (there, o * N_INNER + (p + sign) % N_INNER)
        for device, there in first
        for o, p in [divmod(device, N_INNER)]
    ]
    return lax.ppermute(lax.ppermute(block, AXES, first), AXES, ends)


def unit_of(ref):
    values = ref[...].astype(jnp.float32)
    inv = lax.rsqrt(jnp.sum(values * values, axis=-1, keepdims=True) + NORM_EPS)
    return (values * inv).astype(jnp.bfloat16)


def score(img, txt, pos, text_start, head, stats):
    cosine = lax.dot_general(
        img, txt, (((1,), (1,)), ((), ())), preferred_element_type=jnp.float32
    )
    logit = head[0] * cosine + head[1]
    ids = text_start + lax.broadcasted_iota(jnp.int32, cosine.shape, 1)
    hit = pos == ids
    z = jnp.where(hit, -logit, logit)
    tail = jnp.exp(-jnp.abs(z))
    loss = jnp.maximum(z, 0.0) + jnp.log1p(tail)
    sig = jnp.where(z >= 0.0, 1.0, tail) / (1.0 + tail)
    slope = jnp.where(hit, -sig, sig)
    for row, term in enumerate((loss, slope * cosine, slope)):
        col = jnp.sum(term, axis=0, keepdims=True)
        width = stats.shape[1]
        part = col[:, :width]
        for at in range(width, col.shape[1], width):
            part = part + col[:, at : at + width]
        stats[row : row + 1, :] += part
    return slope.astype(jnp.bfloat16)


def times(a, b):
    return jnp.dot(a, b, preferred_element_type=jnp.float32)


def times_t(a, b):
    return lax.dot_general(a, b, (((0,), (0,)), ((), ())), preferred_element_type=jnp.float32)


def unit_kernel(head, start, img_raw, txt_raw, img_u, txt_u):
    img_u[...] = unit_of(img_raw)
    txt_u[...] = unit_of(txt_raw)


def first_kernel(head, start, img_u, txt_u, pos, img_acc, txt_acc, stats):
    stats[...] = jnp.zeros_like(stats)
    s = score(img_u[...], txt_u[...], pos[...], start[0], head, stats)
    img_acc[...] = times(s, txt_u[...])
    txt_acc[...] = times_t(s, img_u[...])


def second_kernel(
    head, start, img_u, txt_u, far_u, img2_u, pos, pos2, img_in, txt_in, stats_in,
    img_acc, img2_acc, txt_acc, far_acc, stats,
):
    stats[...] = stats_in[...]
    s = score(img_u[...], far_u[...], pos[...], start[2], head, stats)
    s2 = score(img2_u[...], far_u[...], pos2[...], start[2], head, stats)
    s0 = score(img2_u[...], txt_u[...], pos2[...], start[0], head, stats)
    far_acc[...] = times_t(s, img_u[...]) + times_t(s2, img2_u[...])
    img_acc[...] = img_in[...] + times(s, far_u[...])
    img2_acc[...] = times(s2, far_u[...]) + times(s0, txt_u[...])
    txt_acc[...] = txt_in[...] + times_t(s0, img2_u[...])


def third_kernel(head, start, img_u, img2_u, mid_raw, pos, pos2, stats_in, mid_u, slope, slope2, mid_acc, stats):
    stats[...] = stats_in[...]
    mid = unit_of(mid_raw)
    mid_u[...] = mid
    s = score(img_u[...], mid, pos[...], start[1], head, stats)
    s2 = score(img2_u[...], mid, pos2[...], start[1], head, stats)
    slope[...] = s
    slope2[...] = s2
    total = times_t(s, img_u[...]) + times_t(s2, img2_u[...])
    mid_acc[...] = SEND_SCALE * total


def fourth_kernel(head, start, mid_u, slope, slope2, img_in, img2_in, img_acc, img2_acc):
    img_acc[...] = img_in[...] + times(slope[...], mid_u[...])
    total = img2_in[...] + times(slope2[...], mid_u[...])
    img2_acc[...] = SEND_SCALE * total


def finish_kernel(head, start, img_raw, txt_raw, img_total, txt_total, img_grad, txt_grad):
    for raw, total, out in ((img_raw, img_total, img_grad), (txt_raw, txt_total, txt_grad)):
        values = raw[...].astype(jnp.float32)
        inv = lax.rsqrt(jnp.sum(values * values, axis=-1, keepdims=True) + NORM_EPS)
        unit = values * inv
        grad = head[0] * total[...]
        out[...] = inv * (grad - unit * jnp.sum(unit * grad, axis=-1, keepdims=True))


def call(kernel, ins, outs):
    scalars = [pl.BlockSpec(memory_space=pltpu.SMEM)] * 2
    arrays = [pl.BlockSpec(memory_space=pltpu.VMEM)] * (len(ins) - 2)
    return pl.pallas_call(
        kernel,
        in_specs=scalars + arrays,
        out_specs=[pl.BlockSpec(memory_space=pltpu.VMEM)] * len(outs),
        out_shape=outs,
        compiler_params=pltpu.CompilerParams(vmem_limit_bytes=VMEM_LIMIT),
    )(*ins)


def sum_first(s):
    s = jnp.sum(lax.all_gather(s, "z"), axis=0)
    s = jnp.sum(lax.all_gather(s, "x"), axis=0)
    return lax.psum(s, ("y_lo", "core"))


def sum_last(s):
    route = [(device, device ^ 1) for device in range(N_OUTER * N_INNER)]
    return s + lax.ppermute(s, AXES, route)


def shards(image_emb, text_emb, positive, log_scale, logit_bias):
    rows, width = image_emb.shape
    f32, bf16 = jnp.float32, jnp.bfloat16
    temp_scale = jnp.exp(log_scale[0])
    head = jnp.stack([temp_scale, logit_bias[0]])
    device = lax.axis_index(AXES)
    outer_pos, inner_pos = device // N_INNER, device % N_INNER
    start = jnp.stack(
        [(outer_pos * N_INNER + (inner_pos - b) % N_INNER) * rows for b in range(IN_SPAN)]
    ).astype(jnp.int32)
    pos = positive.reshape(rows, 1)
    wide = jax.ShapeDtypeStruct((rows, width), f32)
    unit = jax.ShapeDtypeStruct((rows, width), bf16)
    pair = jax.ShapeDtypeStruct((rows, rows), bf16)
    sums = jax.ShapeDtypeStruct((8, 128), f32)

    mid_raw = one_step_in_two(text_emb, 1)
    pos2 = moved(positive, -1, 0).reshape(rows, 1)
    img_u, txt_u = call(unit_kernel, (head, start, image_emb, text_emb), [unit, unit])
    img2_u = moved(img_u, -1, 0)
    far_u = moved(txt_u, 0, 2)
    img_acc, txt_acc, stats = call(
        first_kernel, (head, start, img_u, txt_u, pos), [wide, wide, sums]
    )
    img_acc, img2_acc, txt_acc, far_acc, stats = call(
        second_kernel,
        (head, start, img_u, txt_u, far_u, img2_u, pos, pos2, img_acc, txt_acc, stats),
        [wide, wide, wide, wide, sums],
    )
    far_back = moved(far_acc, 0, -2)
    mid_u, slope, slope2, mid_acc, stats = call(
        third_kernel,
        (head, start, img_u, img2_u, mid_raw, pos, pos2, stats),
        [unit, pair, pair, wide, sums],
    )
    mid_back = moved(mid_acc.astype(jnp.float16), 0, -1)
    img_acc, img2_acc = call(
        fourth_kernel,
        (head, start, mid_u, slope, slope2, img_acc, img2_acc),
        [wide, wide],
    )
    img_back = moved(img2_acc.astype(jnp.float16), 1, 0)
    always = lax.optimization_barrier(jnp.bool_(True))
    stats = lax.cond(always, sum_first, jnp.zeros_like, stats)
    stats, far_back, mid_back, img_back = lax.optimization_barrier(
        (stats, far_back, mid_back, img_back)
    )
    totals = jnp.sum(sum_last(stats), axis=1)

    img_total = img_acc + img_back.astype(f32) * (1.0 / SEND_SCALE)
    txt_total = txt_acc + far_back + mid_back.astype(f32) * (1.0 / SEND_SCALE)
    image_grad, text_grad = call(
        finish_kernel,
        (head, start, image_emb, text_emb, img_total, txt_total),
        [wide, wide],
    )
    pair_count = f32(rows * N_OUTER * N_INNER * 2 * IN_SPAN * rows)
    loss = (totals[0] / pair_count).reshape(1)
    head_grad = jnp.stack([temp_scale * totals[1], totals[2]]) / pair_count
    return (image_grad, text_grad, loss, head_grad)


def solution(mesh):
    fine = Mesh(mesh.devices.reshape(SIZES), AXES)
    return jax.shard_map(
        shards,
        mesh=fine,
        in_specs=(P(AXES, None), P(AXES, None), P(AXES), P(), P()),
        out_specs=(P(AXES, None), P(AXES, None), P(), P()),
        check_vma=False,
    )
```

```python
import jax
import jax.numpy as jnp
from jax import lax
from jax.experimental import pallas as pl
from jax.experimental.pallas import tpu as pltpu
from jax.sharding import Mesh
from jax.sharding import PartitionSpec as P

IN_SPAN = 3
NORM_EPS = 1e-06
AXES = ("y_lo", "core", "z", "x", "y_hi")
SIZES = (4, 2, 12, 4, 2)
N_OUTER, N_INNER = 8, 96
SEND_SCALE = 64.0
VMEM_LIMIT = 14 * 1024 * 1024


def moved(block, outer_step, inner_step):
    route = [
        (o * N_INNER + p, (o + outer_step) % N_OUTER * N_INNER + (p + inner_step) % N_INNER)
        for o in range(N_OUTER)
        for p in range(N_INNER)
    ]
    return lax.ppermute(block, AXES, route)


def half_way():
    route = []
    for device in range(N_OUTER * N_INNER):
        o, p = divmod(device, N_INNER)
        y = p % 2 * 4 + o // 2
        y = (y + (2 if o % 2 == 0 else 6)) % 8
        route.append((device, (y % 4 * 2 + o % 2) * N_INNER + p // 2 * 2 + y // 4))
    return route


def one_step_in_two(block, sign):
    first = half_way()
    ends = [
        (there, o * N_INNER + (p + sign) % N_INNER)
        for device, there in first
        for o, p in [divmod(device, N_INNER)]
    ]
    return lax.ppermute(lax.ppermute(block, AXES, first), AXES, ends)


def unit_of(ref):
    values = ref[...].astype(jnp.float32)
    inv = lax.rsqrt(jnp.sum(values * values, axis=-1, keepdims=True) + NORM_EPS)
    return (values * inv).astype(jnp.bfloat16)


def score(img, txt, pos, text_start, head, stats):
    cosine = lax.dot_general(
        img, txt, (((1,), (1,)), ((), ())), preferred_element_type=jnp.float32
    )
    logit = head[0] * cosine + head[1]
    ids = text_start + lax.broadcasted_iota(jnp.int32, cosine.shape, 1)
    hit = pos == ids
    z = jnp.where(hit, -logit, logit)
    tail = jnp.exp(-jnp.abs(z))
    loss = jnp.maximum(z, 0.0) + jnp.log1p(tail)
    sig = jnp.where(z >= 0.0, 1.0, tail) / (1.0 + tail)
    slope = jnp.where(hit, -sig, sig)
    for row, term in enumerate((loss, slope * cosine, slope)):
        col = jnp.sum(term, axis=0, keepdims=True)
        width = stats.shape[1]
        part = col[:, :width]
        for at in range(width, col.shape[1], width):
            part = part + col[:, at : at + width]
        stats[row : row + 1, :] += part
    return slope.astype(jnp.bfloat16)


def times(a, b):
    return jnp.dot(a, b, preferred_element_type=jnp.float32)


def times_t(a, b):
    return lax.dot_general(a, b, (((0,), (0,)), ((), ())), preferred_element_type=jnp.float32)


def unit_kernel(head, start, img_raw, txt_raw, img_u, txt_u):
    img_u[...] = unit_of(img_raw)
    txt_u[...] = unit_of(txt_raw)


def first_kernel(head, start, img_u, txt_u, pos, img_acc, txt_acc, stats):
    stats[...] = jnp.zeros_like(stats)
    s = score(img_u[...], txt_u[...], pos[...], start[0], head, stats)
    img_acc[...] = times(s, txt_u[...])
    txt_acc[...] = times_t(s, img_u[...])


def second_kernel(
    head, start, img_u, txt_u, far_u, img2_u, pos, pos2, img_in, txt_in, stats_in,
    img_acc, img2_acc, txt_acc, far_acc, stats,
):
    stats[...] = stats_in[...]
    s = score(img_u[...], far_u[...], pos[...], start[2], head, stats)
    s2 = score(img2_u[...], far_u[...], pos2[...], start[2], head, stats)
    s0 = score(img2_u[...], txt_u[...], pos2[...], start[0], head, stats)
    far_acc[...] = times_t(s, img_u[...]) + times_t(s2, img2_u[...])
    img_acc[...] = img_in[...] + times(s, far_u[...])
    img2_acc[...] = times(s2, far_u[...]) + times(s0, txt_u[...])
    txt_acc[...] = txt_in[...] + times_t(s0, img2_u[...])


def third_kernel(head, start, img_u, img2_u, mid_raw, pos, pos2, stats_in, mid_u, slope, slope2, mid_acc, stats):
    stats[...] = stats_in[...]
    mid = unit_of(mid_raw)
    mid_u[...] = mid
    s = score(img_u[...], mid, pos[...], start[1], head, stats)
    s2 = score(img2_u[...], mid, pos2[...], start[1], head, stats)
    slope[...] = s
    slope2[...] = s2
    total = times_t(s, img_u[...]) + times_t(s2, img2_u[...])
    mid_acc[...] = SEND_SCALE * total


def fourth_kernel(head, start, mid_u, slope, slope2, img_in, img2_in, img_acc, img2_acc):
    img_acc[...] = img_in[...] + times(slope[...], mid_u[...])
    total = img2_in[...] + times(slope2[...], mid_u[...])
    img2_acc[...] = SEND_SCALE * total


def finish_kernel(head, start, img_raw, txt_raw, img_total, txt_total, img_grad, txt_grad):
    for raw, total, out in ((img_raw, img_total, img_grad), (txt_raw, txt_total, txt_grad)):
        values = raw[...].astype(jnp.float32)
        inv = lax.rsqrt(jnp.sum(values * values, axis=-1, keepdims=True) + NORM_EPS)
        unit = values * inv
        grad = head[0] * total[...]
        out[...] = inv * (grad - unit * jnp.sum(unit * grad, axis=-1, keepdims=True))


def call(kernel, ins, outs):
    scalars = [pl.BlockSpec(memory_space=pltpu.SMEM)] * 2
    arrays = [pl.BlockSpec(memory_space=pltpu.VMEM)] * (len(ins) - 2)
    return pl.pallas_call(
        kernel,
        in_specs=scalars + arrays,
        out_specs=[pl.BlockSpec(memory_space=pltpu.VMEM)] * len(outs),
        out_shape=outs,
        compiler_params=pltpu.CompilerParams(vmem_limit_bytes=VMEM_LIMIT),
    )(*ins)


def sum_z(s):
    return jnp.sum(lax.all_gather(s, "z"), axis=0)


def sum_x_y_lo(s):
    return lax.psum(jnp.sum(lax.all_gather(s, "x"), axis=0), ("y_lo", "core"))


def sum_last(s):
    route = [(device, device ^ 1) for device in range(N_OUTER * N_INNER)]
    return s + lax.ppermute(s, AXES, route)


def shards(image_emb, text_emb, positive, log_scale, logit_bias):
    rows, width = image_emb.shape
    f32, bf16 = jnp.float32, jnp.bfloat16
    temp_scale = jnp.exp(log_scale[0])
    head = jnp.stack([temp_scale, logit_bias[0]])
    device = lax.axis_index(AXES)
    outer_pos, inner_pos = device // N_INNER, device % N_INNER
    start = jnp.stack(
        [(outer_pos * N_INNER + (inner_pos - b) % N_INNER) * rows for b in range(IN_SPAN)]
    ).astype(jnp.int32)
    pos = positive.reshape(rows, 1)
    wide = jax.ShapeDtypeStruct((rows, width), f32)
    unit = jax.ShapeDtypeStruct((rows, width), bf16)
    pair = jax.ShapeDtypeStruct((rows, rows), bf16)
    sums = jax.ShapeDtypeStruct((8, 128), f32)

    mid_raw = one_step_in_two(text_emb, 1)
    pos2 = moved(positive, -1, 0).reshape(rows, 1)
    img_u, txt_u = call(unit_kernel, (head, start, image_emb, text_emb), [unit, unit])
    img2_u = moved(img_u, -1, 0)
    far_u = moved(txt_u, 0, 2)
    img_acc, txt_acc, stats = call(
        first_kernel, (head, start, img_u, txt_u, pos), [wide, wide, sums]
    )
    img_acc, img2_acc, txt_acc, far_acc, stats = call(
        second_kernel,
        (head, start, img_u, txt_u, far_u, img2_u, pos, pos2, img_acc, txt_acc, stats),
        [wide, wide, wide, wide, sums],
    )
    far_back = moved((SEND_SCALE * far_acc).astype(jnp.float16), 0, -2)
    mid_u, slope, slope2, mid_acc, stats = call(
        third_kernel,
        (head, start, img_u, img2_u, mid_raw, pos, pos2, stats),
        [unit, pair, pair, wide, sums],
    )
    img_acc, img2_acc = call(
        fourth_kernel,
        (head, start, mid_u, slope, slope2, img_acc, img2_acc),
        [wide, wide],
    )
    always = lax.optimization_barrier(jnp.bool_(True))
    stats = lax.cond(always, sum_z, jnp.zeros_like, stats)
    stats, mid_half, img_half = lax.optimization_barrier(
        (stats, mid_acc.astype(jnp.float16), img2_acc.astype(jnp.float16))
    )
    mid_back = moved(mid_half, 0, -1)
    img_back = moved(img_half, 1, 0)
    stats = lax.cond(always, sum_x_y_lo, jnp.zeros_like, stats)
    stats, far_back, mid_back, img_back = lax.optimization_barrier(
        (stats, far_back, mid_back, img_back)
    )
    totals = jnp.sum(sum_last(stats), axis=1)

    img_total = img_acc + img_back.astype(f32) * (1.0 / SEND_SCALE)
    txt_total = txt_acc + (far_back.astype(f32) + mid_back.astype(f32)) * (1.0 / SEND_SCALE)
    image_grad, text_grad = call(
        finish_kernel,
        (head, start, image_emb, text_emb, img_total, txt_total),
        [wide, wide],
    )
    pair_count = f32(rows * N_OUTER * N_INNER * 2 * IN_SPAN * rows)
    loss = (totals[0] / pair_count).reshape(1)
    head_grad = jnp.stack([temp_scale * totals[1], totals[2]]) / pair_count
    return (image_grad, text_grad, loss, head_grad)


def solution(mesh):
    fine = Mesh(mesh.devices.reshape(SIZES), AXES)
    return jax.shard_map(
        shards,
        mesh=fine,
        in_specs=(P(AXES, None), P(AXES, None), P(AXES), P(), P()),
        out_specs=(P(AXES, None), P(AXES, None), P(), P()),
        check_vma=False,
    )
```

```python
import jax
import jax.numpy as jnp
from jax import lax
from jax.experimental import pallas as pl
from jax.experimental.pallas import tpu as pltpu
from jax.sharding import Mesh
from jax.sharding import PartitionSpec as P

IN_SPAN = 3
NORM_EPS = 1e-06
AXES = ("y_lo", "core", "z", "x", "y_hi")
SIZES = (4, 2, 12, 4, 2)
N_OUTER, N_INNER = 8, 96
SEND_SCALE = 64.0
CODE = 128
VMEM_LIMIT = 14 * 1024 * 1024


def moved(block, outer_step, inner_step):
    route = [
        (o * N_INNER + p, (o + outer_step) % N_OUTER * N_INNER + (p + inner_step) % N_INNER)
        for o in range(N_OUTER)
        for p in range(N_INNER)
    ]
    return lax.ppermute(block, AXES, route)


def half_way():
    route = []
    for device in range(N_OUTER * N_INNER):
        o, p = divmod(device, N_INNER)
        y = p % 2 * 4 + o // 2
        y = (y + (2 if o % 2 == 0 else 6)) % 8
        route.append((device, (y % 4 * 2 + o % 2) * N_INNER + p // 2 * 2 + y // 4))
    return route


def one_step_in_two(block, sign):
    first = half_way()
    ends = [
        (there, o * N_INNER + (p + sign) % N_INNER)
        for device, there in first
        for o, p in [divmod(device, N_INNER)]
    ]
    return lax.ppermute(lax.ppermute(block, AXES, first), AXES, ends)


def unit_of(ref):
    values = ref[...].astype(jnp.float32)
    inv = lax.rsqrt(jnp.sum(values * values, axis=-1, keepdims=True) + NORM_EPS)
    return (values * inv).astype(jnp.bfloat16)


def score(img, txt, pos, text_start, head, stats):
    cosine = lax.dot_general(
        img, txt, (((1,), (1,)), ((), ())), preferred_element_type=jnp.float32
    )
    logit = head[0] * cosine + head[1]
    ids = text_start + lax.broadcasted_iota(jnp.int32, cosine.shape, 1)
    hit = pos == ids
    z = jnp.where(hit, -logit, logit)
    tail = jnp.exp(-jnp.abs(z))
    loss = jnp.maximum(z, 0.0) + jnp.log1p(tail)
    sig = jnp.where(z >= 0.0, 1.0, tail) / (1.0 + tail)
    slope = jnp.where(hit, -sig, sig)
    for row, term in enumerate((loss, slope * cosine, slope)):
        col = jnp.sum(term, axis=0, keepdims=True)
        width = stats.shape[1]
        part = col[:, :width]
        for at in range(width, col.shape[1], width):
            part = part + col[:, at : at + width]
        stats[row : row + 1, :] += part
    return slope.astype(jnp.bfloat16)


def times(a, b):
    return jnp.dot(a, b, preferred_element_type=jnp.float32)


def times_t(a, b):
    return lax.dot_general(a, b, (((0,), (0,)), ((), ())), preferred_element_type=jnp.float32)


def unit_kernel(head, start, img_raw, txt_raw, pos, img_u, txt_u):
    width = txt_u.shape[1]
    img_u[:, :width] = unit_of(img_raw)
    txt_u[...] = unit_of(txt_raw)
    lane = lax.broadcasted_iota(jnp.int32, (pos.shape[0], CODE), 1)
    index = pos[...]
    code = jnp.where(lane == 0, index & 255, (index >> 8) & 255)
    code = jnp.where(lane == 2, index >> 16, code)
    img_u[:, width:] = code.astype(jnp.float32).astype(jnp.bfloat16)


def decoded(img2, width):
    code = img2[:, width:].astype(jnp.float32)
    index = code[:, 0:1] + 256.0 * code[:, 1:2] + 65536.0 * code[:, 2:3]
    return img2[:, :width], index.astype(jnp.int32)


def first_kernel(head, start, img_u, txt_u, pos, slope, stats):
    stats[...] = jnp.zeros_like(stats)
    img = img_u[:, : txt_u.shape[1]]
    slope[...] = score(img, txt_u[...], pos[...], start[0], head, stats)


def second_kernel(
    head, start, img_u, txt_u, far_u, img2_u, pos, slope, stats_in,
    img_acc, img2_acc, txt_acc, far_acc, stats,
):
    stats[...] = stats_in[...]
    img = img_u[:, : txt_u.shape[1]]
    img2, pos2 = decoded(img2_u, txt_u.shape[1])
    s = score(img, far_u[...], pos[...], start[2], head, stats)
    s2 = score(img2, far_u[...], pos2, start[2], head, stats)
    s0 = score(img2, txt_u[...], pos2, start[0], head, stats)
    far_acc[...] = SEND_SCALE * (times_t(s, img) + times_t(s2, img2))
    img_acc[...] = times(slope[...], txt_u[...]) + times(s, far_u[...])
    img2_acc[...] = times(s2, far_u[...]) + times(s0, txt_u[...])
    txt_acc[...] = times_t(slope[...], img) + times_t(s0, img2)


def third_kernel(head, start, img_u, img2_u, mid_raw, pos, stats_in, mid_u, slope, slope2, mid_acc, stats):
    stats[...] = stats_in[...]
    mid = unit_of(mid_raw)
    mid_u[...] = mid
    img = img_u[:, : mid.shape[1]]
    img2, pos2 = decoded(img2_u, mid.shape[1])
    s = score(img, mid, pos[...], start[1], head, stats)
    s2 = score(img2, mid, pos2, start[1], head, stats)
    slope[...] = s
    slope2[...] = s2
    mid_acc[...] = SEND_SCALE * (times_t(s, img) + times_t(s2, img2))


def fourth_kernel(head, start, mid_u, slope, slope2, img_in, img2_in, img_acc, img2_acc):
    img_acc[...] = img_in[...] + times(slope[...], mid_u[...])
    total = img2_in[...] + times(slope2[...], mid_u[...])
    img2_acc[...] = SEND_SCALE * total


def finish_kernel(head, start, img_raw, txt_raw, img_total, txt_total, img_grad, txt_grad):
    for raw, total, out in ((img_raw, img_total, img_grad), (txt_raw, txt_total, txt_grad)):
        values = raw[...].astype(jnp.float32)
        inv = lax.rsqrt(jnp.sum(values * values, axis=-1, keepdims=True) + NORM_EPS)
        unit = values * inv
        grad = head[0] * total[...]
        out[...] = inv * (grad - unit * jnp.sum(unit * grad, axis=-1, keepdims=True))


def call(kernel, ins, outs):
    scalars = [pl.BlockSpec(memory_space=pltpu.SMEM)] * 2
    arrays = [pl.BlockSpec(memory_space=pltpu.VMEM)] * (len(ins) - 2)
    return pl.pallas_call(
        kernel,
        in_specs=scalars + arrays,
        out_specs=[pl.BlockSpec(memory_space=pltpu.VMEM)] * len(outs),
        out_shape=outs,
        compiler_params=pltpu.CompilerParams(vmem_limit_bytes=VMEM_LIMIT),
    )(*ins)


def sum_z(s):
    return jnp.sum(lax.all_gather(s, "z"), axis=0)


def sum_x_y_lo(s):
    return lax.psum(jnp.sum(lax.all_gather(s, "x"), axis=0), ("y_lo", "core"))


def sum_last(s):
    route = [(device, device ^ 1) for device in range(N_OUTER * N_INNER)]
    return s + lax.ppermute(s, AXES, route)


def shards(image_emb, text_emb, positive, log_scale, logit_bias):
    rows, width = image_emb.shape
    f32, bf16 = jnp.float32, jnp.bfloat16
    temp_scale = jnp.exp(log_scale[0])
    head = jnp.stack([temp_scale, logit_bias[0]])
    device = lax.axis_index(AXES)
    outer_pos, inner_pos = device // N_INNER, device % N_INNER
    start = jnp.stack(
        [(outer_pos * N_INNER + (inner_pos - b) % N_INNER) * rows for b in range(IN_SPAN)]
    ).astype(jnp.int32)
    pos = positive.reshape(rows, 1)
    wide = jax.ShapeDtypeStruct((rows, width), f32)
    unit = jax.ShapeDtypeStruct((rows, width), bf16)
    pair = jax.ShapeDtypeStruct((rows, rows), bf16)
    sums = jax.ShapeDtypeStruct((8, 128), f32)

    mid_raw = one_step_in_two(text_emb, 1)
    marked = jax.ShapeDtypeStruct((rows, width + CODE), bf16)
    img_u, txt_u = call(unit_kernel, (head, start, image_emb, text_emb, pos), [marked, unit])
    img2_u = moved(img_u, -1, 0)
    far_u = moved(txt_u, 0, 2)
    slope, stats = call(first_kernel, (head, start, img_u, txt_u, pos), [pair, sums])
    img_acc, img2_acc, txt_acc, far_acc, stats = call(
        second_kernel,
        (head, start, img_u, txt_u, far_u, img2_u, pos, slope, stats),
        [wide, wide, wide, wide, sums],
    )
    mid_u, slope, slope2, mid_acc, stats = call(
        third_kernel,
        (head, start, img_u, img2_u, mid_raw, pos, stats),
        [unit, pair, pair, wide, sums],
    )
    img_acc, img2_acc = call(
        fourth_kernel,
        (head, start, mid_u, slope, slope2, img_acc, img2_acc),
        [wide, wide],
    )
    always = lax.optimization_barrier(jnp.bool_(True))
    stats = lax.cond(always, sum_z, jnp.zeros_like, stats)
    half = jnp.float16
    stats, mid_half, img_half, far_half = lax.optimization_barrier(
        (stats, mid_acc.astype(half), img2_acc.astype(half), far_acc.astype(half))
    )
    mid_back = moved(mid_half, 0, -1)
    img_back = moved(img_half, 1, 0)
    far_back = moved(far_half, 0, -2)
    stats = lax.cond(always, sum_x_y_lo, jnp.zeros_like, stats)
    stats, far_back, mid_back, img_back = lax.optimization_barrier(
        (stats, far_back, mid_back, img_back)
    )
    totals = jnp.sum(sum_last(stats), axis=1)

    img_total = img_acc + img_back.astype(f32) * (1.0 / SEND_SCALE)
    txt_total = txt_acc + (far_back.astype(f32) + mid_back.astype(f32)) * (1.0 / SEND_SCALE)
    image_grad, text_grad = call(
        finish_kernel,
        (head, start, image_emb, text_emb, img_total, txt_total),
        [wide, wide],
    )
    pair_count = f32(rows * N_OUTER * N_INNER * 2 * IN_SPAN * rows)
    loss = (totals[0] / pair_count).reshape(1)
    head_grad = jnp.stack([temp_scale * totals[1], totals[2]]) / pair_count
    return (image_grad, text_grad, loss, head_grad)


def solution(mesh):
    fine = Mesh(mesh.devices.reshape(SIZES), AXES)
    return jax.shard_map(
        shards,
        mesh=fine,
        in_specs=(P(AXES, None), P(AXES, None), P(AXES), P(), P()),
        out_specs=(P(AXES, None), P(AXES, None), P(), P()),
        check_vma=False,
    )
```

```python
import jax
import jax.numpy as jnp
from jax import lax
from jax.experimental import pallas as pl
from jax.experimental.pallas import tpu as pltpu
from jax.sharding import Mesh
from jax.sharding import PartitionSpec as P

IN_SPAN = 3
NORM_EPS = 1e-06
AXES = ("y_lo", "core", "z", "x", "y_hi")
SIZES = (4, 2, 12, 4, 2)
N_OUTER, N_INNER = 8, 96
SEND_SCALE = 64.0
CODE = 128
VMEM_LIMIT = 14 * 1024 * 1024


def moved(block, outer_step, inner_step):
    route = [
        (o * N_INNER + p, (o + outer_step) % N_OUTER * N_INNER + (p + inner_step) % N_INNER)
        for o in range(N_OUTER)
        for p in range(N_INNER)
    ]
    return lax.ppermute(block, AXES, route)


def half_way():
    route = []
    for device in range(N_OUTER * N_INNER):
        o, p = divmod(device, N_INNER)
        y = p % 2 * 4 + o // 2
        y = (y + (2 if o % 2 == 0 else 6)) % 8
        route.append((device, (y % 4 * 2 + o % 2) * N_INNER + p // 2 * 2 + y // 4))
    return route


def one_step_in_two(block, sign):
    first = half_way()
    ends = [
        (there, o * N_INNER + (p + sign) % N_INNER)
        for device, there in first
        for o, p in [divmod(device, N_INNER)]
    ]
    return lax.ppermute(lax.ppermute(block, AXES, first), AXES, ends)


def unit_of(ref):
    values = ref[...].astype(jnp.float32)
    inv = lax.rsqrt(jnp.sum(values * values, axis=-1, keepdims=True) + NORM_EPS)
    return (values * inv).astype(jnp.bfloat16)


def score(img, txt, pos, text_start, head, stats):
    cosine = lax.dot_general(
        img, txt, (((1,), (1,)), ((), ())), preferred_element_type=jnp.float32
    )
    logit = head[0] * cosine + head[1]
    ids = text_start + lax.broadcasted_iota(jnp.int32, cosine.shape, 1)
    hit = pos == ids
    z = jnp.where(hit, -logit, logit)
    tail = jnp.exp(-jnp.abs(z))
    loss = jnp.maximum(z, 0.0) + jnp.log1p(tail)
    sig = jnp.where(z >= 0.0, 1.0, tail) / (1.0 + tail)
    slope = jnp.where(hit, -sig, sig)
    for row, term in enumerate((loss, slope * cosine, slope)):
        col = jnp.sum(term, axis=0, keepdims=True)
        width = stats.shape[1]
        part = col[:, :width]
        for at in range(width, col.shape[1], width):
            part = part + col[:, at : at + width]
        stats[row : row + 1, :] += part
    return slope.astype(jnp.bfloat16)


def times(a, b):
    return jnp.dot(a, b, preferred_element_type=jnp.float32)


def times_t(a, b):
    return lax.dot_general(a, b, (((0,), (0,)), ((), ())), preferred_element_type=jnp.float32)


def unit_kernel(head, start, img_raw, txt_raw, pos, img_u, txt_u):
    width = txt_u.shape[1]
    img_u[:, :width] = unit_of(img_raw)
    txt_u[...] = unit_of(txt_raw)
    lane = lax.broadcasted_iota(jnp.int32, (pos.shape[0], CODE), 1)
    index = pos[...]
    code = jnp.where(lane == 0, index & 255, (index >> 8) & 255)
    code = jnp.where(lane == 2, index >> 16, code)
    img_u[:, width:] = code.astype(jnp.float32).astype(jnp.bfloat16)


def decoded(img2, width):
    code = img2[:, width:].astype(jnp.float32)
    index = code[:, 0:1] + 256.0 * code[:, 1:2] + 65536.0 * code[:, 2:3]
    return img2[:, :width], index.astype(jnp.int32)


def first_kernel(head, start, img_u, txt_u, pos, slope, stats):
    stats[...] = jnp.zeros_like(stats)
    img = img_u[:, : txt_u.shape[1]]
    slope[...] = score(img, txt_u[...], pos[...], start[0], head, stats)


def second_kernel(
    head, start, img_u, txt_u, far_u, img2_u, pos, slope, stats_in,
    img_acc, img2_acc, txt_acc, far_acc, stats,
):
    stats[...] = stats_in[...]
    img = img_u[:, : txt_u.shape[1]]
    img2, pos2 = decoded(img2_u, txt_u.shape[1])
    s = score(img, far_u[...], pos[...], start[2], head, stats)
    s2 = score(img2, far_u[...], pos2, start[2], head, stats)
    s0 = score(img2, txt_u[...], pos2, start[0], head, stats)
    far_acc[...] = SEND_SCALE * (times_t(s, img) + times_t(s2, img2))
    img_acc[...] = times(slope[...], txt_u[...]) + times(s, far_u[...])
    img2_acc[...] = times(s2, far_u[...]) + times(s0, txt_u[...])
    txt_acc[...] = times_t(slope[...], img) + times_t(s0, img2)


def third_kernel(head, start, img_u, img2_u, mid_raw, pos, stats_in, mid_u, slope, slope2, mid_acc, stats):
    stats[...] = stats_in[...]
    mid = unit_of(mid_raw)
    mid_u[...] = mid
    img = img_u[:, : mid.shape[1]]
    img2, pos2 = decoded(img2_u, mid.shape[1])
    s = score(img, mid, pos[...], start[1], head, stats)
    s2 = score(img2, mid, pos2, start[1], head, stats)
    slope[...] = s
    slope2[...] = s2
    mid_acc[...] = SEND_SCALE * (times_t(s, img) + times_t(s2, img2))


def fourth_kernel(head, start, mid_u, slope, slope2, img_in, img2_in, img_acc, img2_acc):
    img_acc[...] = img_in[...] + times(slope[...], mid_u[...])
    total = img2_in[...] + times(slope2[...], mid_u[...])
    img2_acc[...] = SEND_SCALE * total


def finish_kernel(head, start, img_raw, txt_raw, img_total, txt_total, img_grad, txt_grad):
    for raw, total, out in ((img_raw, img_total, img_grad), (txt_raw, txt_total, txt_grad)):
        values = raw[...].astype(jnp.float32)
        inv = lax.rsqrt(jnp.sum(values * values, axis=-1, keepdims=True) + NORM_EPS)
        unit = values * inv
        grad = head[0] * total[...]
        out[...] = inv * (grad - unit * jnp.sum(unit * grad, axis=-1, keepdims=True))


def call(kernel, ins, outs):
    scalars = [pl.BlockSpec(memory_space=pltpu.SMEM)] * 2
    arrays = [pl.BlockSpec(memory_space=pltpu.VMEM)] * (len(ins) - 2)
    return pl.pallas_call(
        kernel,
        in_specs=scalars + arrays,
        out_specs=[pl.BlockSpec(memory_space=pltpu.VMEM)] * len(outs),
        out_shape=outs,
        compiler_params=pltpu.CompilerParams(vmem_limit_bytes=VMEM_LIMIT),
    )(*ins)


def sum_y_lo(s):
    return lax.psum(s, ("y_lo", "core"))


def sum_z_x(s):
    s = jnp.sum(lax.all_gather(s, "z"), axis=0)
    return jnp.sum(lax.all_gather(s, "x"), axis=0)


def sum_last(s):
    route = [(device, device ^ 1) for device in range(N_OUTER * N_INNER)]
    return s + lax.ppermute(s, AXES, route)


def shards(image_emb, text_emb, positive, log_scale, logit_bias):
    rows, width = image_emb.shape
    f32, bf16 = jnp.float32, jnp.bfloat16
    temp_scale = jnp.exp(log_scale[0])
    head = jnp.stack([temp_scale, logit_bias[0]])
    device = lax.axis_index(AXES)
    outer_pos, inner_pos = device // N_INNER, device % N_INNER
    start = jnp.stack(
        [(outer_pos * N_INNER + (inner_pos - b) % N_INNER) * rows for b in range(IN_SPAN)]
    ).astype(jnp.int32)
    pos = positive.reshape(rows, 1)
    wide = jax.ShapeDtypeStruct((rows, width), f32)
    unit = jax.ShapeDtypeStruct((rows, width), bf16)
    pair = jax.ShapeDtypeStruct((rows, rows), bf16)
    sums = jax.ShapeDtypeStruct((8, 128), f32)

    mid_raw = one_step_in_two(text_emb, 1)
    marked = jax.ShapeDtypeStruct((rows, width + CODE), bf16)
    img_u, txt_u = call(unit_kernel, (head, start, image_emb, text_emb, pos), [marked, unit])
    img2_u = moved(img_u, -1, 0)
    far_u = moved(txt_u, 0, 2)
    slope, stats = call(first_kernel, (head, start, img_u, txt_u, pos), [pair, sums])
    img_acc, img2_acc, txt_acc, far_acc, stats = call(
        second_kernel,
        (head, start, img_u, txt_u, far_u, img2_u, pos, slope, stats),
        [wide, wide, wide, wide, sums],
    )
    mid_u, slope, slope2, mid_acc, stats = call(
        third_kernel,
        (head, start, img_u, img2_u, mid_raw, pos, stats),
        [unit, pair, pair, wide, sums],
    )
    img_acc, img2_acc = call(
        fourth_kernel,
        (head, start, mid_u, slope, slope2, img_acc, img2_acc),
        [wide, wide],
    )
    always = lax.optimization_barrier(jnp.bool_(True))
    stats = lax.cond(always, sum_y_lo, jnp.zeros_like, stats)
    half = jnp.float16
    stats, mid_half, img_half, far_half = lax.optimization_barrier(
        (stats, mid_acc.astype(half), img2_acc.astype(half), far_acc.astype(half))
    )
    far_back = moved(far_half, 0, -2)
    img_back = moved(img_half, 1, 0)
    mid_back = moved(mid_half, 0, -1)
    stats = lax.cond(always, sum_z_x, jnp.zeros_like, stats)
    stats, mid_back, img_back, far_back = lax.optimization_barrier(
        (stats, mid_back, img_back, far_back)
    )
    totals = jnp.sum(sum_last(stats), axis=1)

    img_total = img_acc + img_back.astype(f32) * (1.0 / SEND_SCALE)
    txt_total = txt_acc + (far_back.astype(f32) + mid_back.astype(f32)) * (1.0 / SEND_SCALE)
    image_grad, text_grad = call(
        finish_kernel,
        (head, start, image_emb, text_emb, img_total, txt_total),
        [wide, wide],
    )
    pair_count = f32(rows * N_OUTER * N_INNER * 2 * IN_SPAN * rows)
    loss = (totals[0] / pair_count).reshape(1)
    head_grad = jnp.stack([temp_scale * totals[1], totals[2]]) / pair_count
    return (image_grad, text_grad, loss, head_grad)


def solution(mesh):
    fine = Mesh(mesh.devices.reshape(SIZES), AXES)
    return jax.shard_map(
        shards,
        mesh=fine,
        in_specs=(P(AXES, None), P(AXES, None), P(AXES), P(), P()),
        out_specs=(P(AXES, None), P(AXES, None), P(), P()),
        check_vma=False,
    )
```

```python
import jax
import jax.numpy as jnp
from jax import lax
from jax.experimental import pallas as pl
from jax.experimental.pallas import tpu as pltpu
from jax.sharding import Mesh
from jax.sharding import PartitionSpec as P

IN_SPAN = 3
NORM_EPS = 1e-06
AXES = ("y_lo", "core", "z", "x", "y_hi")
SIZES = (4, 2, 12, 4, 2)
N_OUTER, N_INNER = 8, 96
SEND_SCALE = 64.0
CODE = 128
VMEM_LIMIT = 14 * 1024 * 1024


def moved(block, outer_step, inner_step):
    route = [
        (o * N_INNER + p, (o + outer_step) % N_OUTER * N_INNER + (p + inner_step) % N_INNER)
        for o in range(N_OUTER)
        for p in range(N_INNER)
    ]
    return lax.ppermute(block, AXES, route)


def half_way():
    route = []
    for device in range(N_OUTER * N_INNER):
        o, p = divmod(device, N_INNER)
        y = p % 2 * 4 + o // 2
        y = (y + (2 if o % 2 == 0 else 6)) % 8
        route.append((device, (y % 4 * 2 + o % 2) * N_INNER + p // 2 * 2 + y // 4))
    return route


def second_half(sign):
    return [
        (there, o * N_INNER + (p + sign) % N_INNER)
        for device, there in half_way()
        for o, p in [divmod(device, N_INNER)]
    ]


def unit_of(ref):
    values = ref[...].astype(jnp.float32)
    inv = lax.rsqrt(jnp.sum(values * values, axis=-1, keepdims=True) + NORM_EPS)
    return (values * inv).astype(jnp.bfloat16)


def score(img, txt, pos, text_start, head, stats):
    cosine = lax.dot_general(
        img, txt, (((1,), (1,)), ((), ())), preferred_element_type=jnp.float32
    )
    logit = head[0] * cosine + head[1]
    ids = text_start + lax.broadcasted_iota(jnp.int32, cosine.shape, 1)
    hit = pos == ids
    z = jnp.where(hit, -logit, logit)
    tail = jnp.exp(-jnp.abs(z))
    loss = jnp.maximum(z, 0.0) + jnp.log1p(tail)
    sig = jnp.where(z >= 0.0, 1.0, tail) / (1.0 + tail)
    slope = jnp.where(hit, -sig, sig)
    for row, term in enumerate((loss, slope * cosine, slope)):
        col = jnp.sum(term, axis=0, keepdims=True)
        width = stats.shape[1]
        part = col[:, :width]
        for at in range(width, col.shape[1], width):
            part = part + col[:, at : at + width]
        stats[row : row + 1, :] += part
    return slope.astype(jnp.bfloat16)


def times(a, b):
    return jnp.dot(a, b, preferred_element_type=jnp.float32)


def times_t(a, b):
    return lax.dot_general(a, b, (((0,), (0,)), ((), ())), preferred_element_type=jnp.float32)


def unit_kernel(head, start, img_raw, txt_raw, pos, img_u, txt_u):
    width = txt_u.shape[1]
    img_u[:, :width] = unit_of(img_raw)
    txt_u[...] = unit_of(txt_raw)
    lane = lax.broadcasted_iota(jnp.int32, (pos.shape[0], CODE), 1)
    index = pos[...]
    code = jnp.where(lane == 0, index & 255, (index >> 8) & 255)
    code = jnp.where(lane == 2, index >> 16, code)
    img_u[:, width:] = code.astype(jnp.float32).astype(jnp.bfloat16)


def decoded(img2, width):
    code = img2[:, width:].astype(jnp.float32)
    index = code[:, 0:1] + 256.0 * code[:, 1:2] + 65536.0 * code[:, 2:3]
    return img2[:, :width], index.astype(jnp.int32)


def first_kernel(head, start, img_u, txt_u, pos, slope, stats):
    stats[...] = jnp.zeros_like(stats)
    img = img_u[:, : txt_u.shape[1]]
    slope[...] = score(img, txt_u[...], pos[...], start[0], head, stats)


def second_kernel(
    head, start, img_u, txt_u, far_u, img2_u, pos, slope, stats_in,
    img_acc, img2_acc, txt_acc, far_acc, stats,
):
    stats[...] = stats_in[...]
    img = img_u[:, : txt_u.shape[1]]
    img2, pos2 = decoded(img2_u, txt_u.shape[1])
    s = score(img, far_u[...], pos[...], start[2], head, stats)
    s2 = score(img2, far_u[...], pos2, start[2], head, stats)
    s0 = score(img2, txt_u[...], pos2, start[0], head, stats)
    far_acc[...] = SEND_SCALE * (times_t(s, img) + times_t(s2, img2))
    img_acc[...] = times(slope[...], txt_u[...]) + times(s, far_u[...])
    img2_acc[...] = times(s2, far_u[...]) + times(s0, txt_u[...])
    txt_acc[...] = times_t(slope[...], img) + times_t(s0, img2)


def third_kernel(head, start, img_u, img2_u, mid_raw, pos, stats_in, mid_u, slope, slope2, mid_acc, stats):
    stats[...] = stats_in[...]
    mid = unit_of(mid_raw)
    mid_u[...] = mid
    img = img_u[:, : mid.shape[1]]
    img2, pos2 = decoded(img2_u, mid.shape[1])
    s = score(img, mid, pos[...], start[1], head, stats)
    s2 = score(img2, mid, pos2, start[1], head, stats)
    slope[...] = s
    slope2[...] = s2
    mid_acc[...] = SEND_SCALE * (times_t(s, img) + times_t(s2, img2))


def fourth_kernel(head, start, mid_u, slope, slope2, img_in, img2_in, img_acc, img2_acc):
    img_acc[...] = img_in[...] + times(slope[...], mid_u[...])
    total = img2_in[...] + times(slope2[...], mid_u[...])
    img2_acc[...] = SEND_SCALE * total


def finish_kernel(head, start, img_raw, txt_raw, img_total, txt_total, img_grad, txt_grad):
    for raw, total, out in ((img_raw, img_total, img_grad), (txt_raw, txt_total, txt_grad)):
        values = raw[...].astype(jnp.float32)
        inv = lax.rsqrt(jnp.sum(values * values, axis=-1, keepdims=True) + NORM_EPS)
        unit = values * inv
        grad = head[0] * total[...]
        out[...] = inv * (grad - unit * jnp.sum(unit * grad, axis=-1, keepdims=True))


def call(kernel, ins, outs):
    scalars = [pl.BlockSpec(memory_space=pltpu.SMEM)] * 2
    arrays = [pl.BlockSpec(memory_space=pltpu.VMEM)] * (len(ins) - 2)
    return pl.pallas_call(
        kernel,
        in_specs=scalars + arrays,
        out_specs=[pl.BlockSpec(memory_space=pltpu.VMEM)] * len(outs),
        out_shape=outs,
        compiler_params=pltpu.CompilerParams(vmem_limit_bytes=VMEM_LIMIT),
    )(*ins)


def sum_z(s):
    return jnp.sum(lax.all_gather(s, "z"), axis=0)


def sum_x_y_lo(s):
    return lax.psum(jnp.sum(lax.all_gather(s, "x"), axis=0), ("y_lo", "core"))


def sum_last(s):
    route = [(device, device ^ 1) for device in range(N_OUTER * N_INNER)]
    return s + lax.ppermute(s, AXES, route)


def shards(image_emb, text_emb, positive, log_scale, logit_bias):
    rows, width = image_emb.shape
    f32, bf16 = jnp.float32, jnp.bfloat16
    temp_scale = jnp.exp(log_scale[0])
    head = jnp.stack([temp_scale, logit_bias[0]])
    device = lax.axis_index(AXES)
    outer_pos, inner_pos = device // N_INNER, device % N_INNER
    start = jnp.stack(
        [(outer_pos * N_INNER + (inner_pos - b) % N_INNER) * rows for b in range(IN_SPAN)]
    ).astype(jnp.int32)
    pos = positive.reshape(rows, 1)
    wide = jax.ShapeDtypeStruct((rows, width), f32)
    unit = jax.ShapeDtypeStruct((rows, width), bf16)
    pair = jax.ShapeDtypeStruct((rows, rows), bf16)
    sums = jax.ShapeDtypeStruct((8, 128), f32)

    mid_raw = lax.ppermute(text_emb, AXES, half_way())
    mid_raw = lax.ppermute(mid_raw, AXES, second_half(1))
    marked = jax.ShapeDtypeStruct((rows, width + CODE), bf16)
    img_u, txt_u = call(unit_kernel, (head, start, image_emb, text_emb, pos), [marked, unit])
    img2_u = moved(img_u, -1, 0)
    far_u = moved(txt_u, 0, 2)
    slope, stats = call(first_kernel, (head, start, img_u, txt_u, pos), [pair, sums])
    img_acc, img2_acc, txt_acc, far_acc, stats = call(
        second_kernel,
        (head, start, img_u, txt_u, far_u, img2_u, pos, slope, stats),
        [wide, wide, wide, wide, sums],
    )
    mid_u, slope, slope2, mid_acc, stats = call(
        third_kernel,
        (head, start, img_u, img2_u, mid_raw, pos, stats),
        [unit, pair, pair, wide, sums],
    )
    img_acc, img2_acc = call(
        fourth_kernel,
        (head, start, mid_u, slope, slope2, img_acc, img2_acc),
        [wide, wide],
    )
    always = lax.optimization_barrier(jnp.bool_(True))
    half = jnp.float16
    mid_back = lax.ppermute(mid_acc.astype(half), AXES, half_way())
    stats = lax.cond(always, sum_z, jnp.zeros_like, stats)
    stats, mid_back, img_back, far_back = lax.optimization_barrier(
        (stats, mid_back, img2_acc.astype(half), far_acc.astype(half))
    )
    mid_back = lax.ppermute(mid_back, AXES, second_half(-1))
    img_back = moved(img_back, 1, 0)
    far_back = moved(far_back, 0, -2)
    stats = lax.cond(always, sum_x_y_lo, jnp.zeros_like, stats)
    stats, mid_back, img_back, far_back = lax.optimization_barrier(
        (stats, mid_back, img_back, far_back)
    )
    totals = jnp.sum(sum_last(stats), axis=1)

    img_total = img_acc + img_back.astype(f32) * (1.0 / SEND_SCALE)
    txt_total = txt_acc + (far_back.astype(f32) + mid_back.astype(f32)) * (1.0 / SEND_SCALE)
    image_grad, text_grad = call(
        finish_kernel,
        (head, start, image_emb, text_emb, img_total, txt_total),
        [wide, wide],
    )
    pair_count = f32(rows * N_OUTER * N_INNER * 2 * IN_SPAN * rows)
    loss = (totals[0] / pair_count).reshape(1)
    head_grad = jnp.stack([temp_scale * totals[1], totals[2]]) / pair_count
    return (image_grad, text_grad, loss, head_grad)


def solution(mesh):
    fine = Mesh(mesh.devices.reshape(SIZES), AXES)
    return jax.shard_map(
        shards,
        mesh=fine,
        in_specs=(P(AXES, None), P(AXES, None), P(AXES), P(), P()),
        out_specs=(P(AXES, None), P(AXES, None), P(), P()),
        check_vma=False,
    )
```
